128 devices in a mesh: row: 16 (over y_lo, x, core), col: 8 (over z, y_hi).
Axes of the slice: x: 4, y: 4 (y_hi: 2, y_lo: 2; y = y_hi * 2 + y_lo), z: 4, core: 2. Of those that a mesh axis runs over, the one named last changes fastest.
Arguments:
- positions: float32 [3, 131072], P(None, ('row', 'col')), may hold values from 0 to 1
- segments: float32 [3, 131072], P(None, ('row', 'col')), may hold values from -1.2 to 1.2
- radius: float32 [131072], P(('row', 'col')), may hold values from 0.05 to 0.2
- currents: float32 [2, 131072], P(None, ('row', 'col')), may hold values from -6 to 6
- resist: float32 [131072], P(('row', 'col')), may hold values from 0.3 to 3
- slot_of: int32 [131072], P(('row', 'col')), may hold values from 0 to 1023, as said below
- pair_list: int32 [4096, 2], P(('row', 'col')), may hold values from 0 to 255, as said below
- near_flag: int32 [4096], P(('row', 'col')), may hold values from 0 to 2, as said below
Outputs:
- voltage: float32 [2, 131072], P(None, ('row', 'col'))
The draws below stay inside these ranges and needn't reach their ends.
Inputs may be any that keep to these rules, and one draw needn't show every extreme that they name: `slot_of`: the elements of shard d hold the values 0 to 1023 once each; a value s puts the element in cluster d * 2 + s // 512. `pair_list`: shard d = r * 8 + c lists 32 slots; each live slot holds a pair (I, J) with I <= J, I in clusters r * 2 * 8 to (r + 1) * 2 * 8 - 1 and (J // 2) % 8 = c; a pair stands in one live slot at most, over all shards. Empty slots hold I = r * 2 * 8 and J = c * 2. `near_flag`: 0 marks an empty slot.
All inputs are finite; a program needn't handle non-finite values.
Results may differ from the reference program's by a relative error of at most 0.0003.
Values sent between devices are 32-bit elements; how exact they have to be, the bound alone decides.
No kernel may reach another device: no remote copies, remote signals or barrier semaphores. Data moves between devices by JAX's collectives and lax.ppermute only.
A program may use at most 64 MiB of HBM per device.

```python
import math
import jax
import jax.numpy as jnp
from jax import lax

CS = 512
CPD = 2
PCAP = 32
NE = 131072
N_ROW = 16
N_COL = 8
DEVICES = 128


def list_layout(key):
    base_key = jax.random.fold_in(key, 7177)
    row_span = CPD * N_COL
    col_span = CPD * N_ROW
    square = row_span * col_span
    device_keys = jax.random.split(base_key, DEVICES)

    def one_device(device_id, device_key):
        row_pos = device_id // N_COL
        col_pos = device_id % N_COL
        candidate = jnp.arange(square, dtype=jnp.int32)
        first_local = candidate // col_span
        second_local = candidate % col_span
        first_id = row_pos * row_span + first_local
        second_id = (second_local // CPD * N_COL + col_pos) * CPD + second_local % CPD
        allowed = second_id >= first_id
        allowed_count = jnp.sum(allowed.astype(jnp.int32))
        key_order, key_jitter, key_near, key_shuffle = jax.random.split(device_key, 4)
        priority = jax.random.permutation(key_order, square).astype(jnp.int32)
        scores = jnp.where(allowed, priority + square, priority)
        _, chosen = lax.top_k(scores, PCAP)
        jitter = jax.random.randint(key_jitter, (), 0, PCAP // 4 + 1)
        wanted = PCAP * (N_ROW - row_pos) // N_ROW - jnp.where(row_pos > 0, jitter, 0)
        live_count = jnp.minimum(allowed_count, jnp.maximum(wanted, 1))
        slot_index = jnp.arange(PCAP, dtype=jnp.int32)
        is_live = slot_index < live_count
        pick_first = jnp.where(is_live, first_id[chosen], row_pos * row_span)
        pick_second = jnp.where(is_live, second_id[chosen], col_pos * CPD)
        near_roll = jax.random.randint(key_near, (PCAP,), 0, 8)
        is_close = pick_second - pick_first < 2 * row_span
        is_near = jnp.where(is_close, near_roll < 4, near_roll < 1)
        flags = jnp.where(is_live, jnp.where(is_near, 2, 1), 0).astype(jnp.int32)
        shuffle = jax.random.permutation(key_shuffle, PCAP)
        pairs = jnp.stack([pick_first, pick_second], 1).astype(jnp.int32)
        return (pairs[shuffle], flags[shuffle])
    pairs, flags = jax.vmap(one_device)(jnp.arange(DEVICES, dtype=jnp.int32), device_keys)
    return (pairs.reshape(DEVICES * PCAP, 2), flags.reshape(DEVICES * PCAP))


def draw_pair_list(key, part):
    pairs, _ = list_layout(key)
    return pairs


def draw_near_flag(key, part):
    _, flags = list_layout(key)
    return flags


def draw_slot_of(key, part):
    per_device = CPD * CS
    device_keys = jax.random.split(jax.random.fold_in(key, 3301), DEVICES)

    def one_device(device_key):
        return jax.random.permutation(device_key, per_device)
    return jax.vmap(one_device)(device_keys).reshape(-1).astype(jnp.int32)


def level_of(stream_key, extent, shards, smallest, top_value):
    def one(dim, shards_of):
        steps = jax.random.uniform(jax.random.fold_in(jax.random.fold_in(stream_key, 6), dim), (shards_of,), jnp.float32, smallest / len(shards), top_value / len(shards))
        return jnp.repeat(jnp.exp(steps), extent[dim] // shards_of).reshape((-1,) + (1,) * (len(extent) - dim - 1))

    factor_of = one(*shards[0])
    for cut in shards[1:]:
        factor_of = factor_of * one(*cut)
    return factor_of


def noise(stream_key, extent, scale, limit, shards=(), kind=jnp.bfloat16):
    gain = level_of(stream_key, extent, shards, -0.22, 0.18) if shards else 1.0
    values = jax.random.normal(stream_key, extent, jnp.float32) * scale * gain
    return jnp.minimum(jnp.maximum(values, -limit), limit).astype(kind)


def setup_inputs(seed: int = 0) -> dict:
    arg_keys = jax.random.split(jax.random.key(seed), 9)
    positions = jnp.clip(1.0 * jax.random.uniform(arg_keys[0], (3, NE), jnp.float32) ** level_of(arg_keys[0], (3, NE), ((1, 128),), -0.2, 0.2), 0.0, 1.0)
    segments = noise(arg_keys[1], (3, NE), 0.2, 1.2, ((1, 128),), jnp.float32)
    radius = jnp.clip(jnp.exp(math.log(0.2) - 1.3862944 * jax.random.uniform(arg_keys[2], (NE,), jnp.float32) ** level_of(arg_keys[2], (NE,), ((0, 128),), -0.2, 0.2)), 0.05, 0.2)
    currents = noise(arg_keys[3], (2, NE), 1.0, 6.0, ((1, 128),), jnp.float32)
    resist = jnp.clip(jnp.exp(math.log(3.0) - 2.3025851 * jax.random.uniform(arg_keys[4], (NE,), jnp.float32) ** level_of(arg_keys[4], (NE,), ((0, 128),), -0.2, 0.2)), 0.3, 3.0)
    slot_of = draw_slot_of(jax.random.fold_in(arg_keys[8], 71), 0)
    pair_list = draw_pair_list(jax.random.fold_in(arg_keys[8], 71), 0)
    near_flag = draw_near_flag(jax.random.fold_in(arg_keys[8], 71), 0)
    return dict(positions=positions, segments=segments, radius=radius, currents=currents, resist=resist, slot_of=slot_of, pair_list=pair_list, near_flag=near_flag)


gauss_step = 0.5 / math.sqrt(3.0)
kernel_gain = 0.25

def tile_block(points_first, vectors_first, radii_first, points_second, vectors_second, radii_second, is_near):
    softening = radii_first[:, None] ** 2 + radii_second[None, :] ** 2
    alignment = vectors_first[0][:, None] * vectors_second[0][None, :]
    for component in (1, 2):
        alignment = alignment + vectors_first[component][:, None] * vectors_second[component][None, :]

    def far_part():
        squared = softening
        for component in range(3):
            squared = squared + (points_first[component][:, None] - points_second[component][None, :]) ** 2
        return 1.0 / jnp.sqrt(squared)

    def near_part():
        summed = jnp.zeros_like(softening)
        for sign_first in (-1.0, 1.0):
            for sign_second in (-1.0, 1.0):
                squared = softening
                for component in range(3):
                    moved_first = points_first[component] + sign_first * gauss_step * vectors_first[component]
                    moved_second = points_second[component] + sign_second * gauss_step * vectors_second[component]
                    squared = squared + (moved_first[:, None] - moved_second[None, :]) ** 2
                summed = summed + 1.0 / jnp.sqrt(squared)
        return 0.25 * summed
    inverse = lax.cond(is_near, near_part, far_part)
    return kernel_gain * alignment * inverse

def reference(positions, segments, radius, currents, resist, slot_of, pair_list, near_flag):
    per_device = CPD * CS
    device_of = jnp.arange(NE, dtype=jnp.int32) // per_device
    global_slot = (device_of * per_device + slot_of).astype(jnp.int32)
    packed = jnp.concatenate([positions, segments, radius[None, :], currents], 0)
    ordered = jnp.zeros_like(packed).at[:, global_slot].set(packed)

    def advance(induced_sum, slot_entry):
        pair_entry, flag_value = slot_entry
        first_id = pair_entry[0].astype(jnp.int32)
        second_id = pair_entry[1].astype(jnp.int32)
        block_first = lax.dynamic_slice_in_dim(ordered, first_id * CS, CS, 1)
        block_second = lax.dynamic_slice_in_dim(ordered, second_id * CS, CS, 1)
        kernel_tile = tile_block(block_first[0:3], block_first[3:6], block_first[6], block_second[0:3], block_second[3:6], block_second[6], flag_value == 2)
        weight_live = (flag_value > 0).astype(induced_sum.dtype)
        weight_mirror = weight_live * (first_id != second_id).astype(induced_sum.dtype)
        direct_part = weight_live * jnp.dot(block_second[7:9], kernel_tile.T, precision=lax.Precision.HIGHEST)
        mirror_part = weight_mirror * jnp.dot(block_first[7:9], kernel_tile, precision=lax.Precision.HIGHEST)
        current = lax.dynamic_slice_in_dim(induced_sum, first_id * CS, CS, 1)
        induced_sum = lax.dynamic_update_slice_in_dim(induced_sum, current + direct_part, first_id * CS, 1)
        current = lax.dynamic_slice_in_dim(induced_sum, second_id * CS, CS, 1)
        induced_sum = lax.dynamic_update_slice_in_dim(induced_sum, current + mirror_part, second_id * CS, 1)
        return (induced_sum, None)
    start_sum = jnp.zeros((2, NE), packed.dtype)
    induced_field, _ = lax.scan(advance, start_sum, (pair_list, near_flag))
    induced = induced_field[:, global_slot]
    voltage_real = resist * currents[0] - induced[1]
    voltage_imag = resist * currents[1] + induced[0]
    return jnp.stack([voltage_real, voltage_imag])
```

```python
import math
import jax
import jax.numpy as jnp
from jax import lax
from jax.experimental import pallas as pl
from jax.experimental.pallas import tpu as pltpu
from jax.sharding import PartitionSpec as P_

CS = 512
G = 0.5 / math.sqrt(3.0)
f32, bf16 = jnp.float32, jnp.bfloat16
M = 128
TN = (((0,), (0,)), ((), ()))
NT = (((1,), (1,)), ((), ()))


def split3(x):
    a = x.astype(bf16).astype(f32)
    r = x - a
    b = r.astype(bf16).astype(f32)
    return a, b, r - b


def rows8():
    return lax.broadcasted_iota(jnp.int32, (8, CS), 0)


def moved(P, L, s):
    if s == 0:
        return P, P[3:4]
    w = (G * L) * (2.0 * s * P + G * L)
    n = P[3:4] + ((w[0:1] + w[1:2]) + w[2:3])
    return P + (s * G) * L, n


def dist_tiles(P, L, s, first):
    Q, n = moved(P, L, s)
    r = rows8()
    if first:
        t = jnp.where(r < 3, -2.0 * Q, jnp.where(r == 3, n, jnp.where(r == 4, 1.0, 0.0)))
    else:
        t = jnp.where(r < 3, Q, jnp.where(r == 3, 1.0, jnp.where(r == 4, n, 0.0)))
    a, b, c = split3(t)
    low = jnp.where(r < 5, 0.0, 1.0)
    if first:
        one = r == 4
        b = jnp.where(one, 1.0, b)
        c = jnp.where(one, 1.0, c)
        a5, b5 = pltpu.roll(a, 5, 0), pltpu.roll(b, 5, 0)
        return [jnp.where(r < 5, a, a5), jnp.where(r < 5, b, a5), jnp.where(r < 5, c, b5)]
    a5, b5, c5 = pltpu.roll(a, 5, 0), pltpu.roll(b, 5, 0), pltpu.roll(c, 5, 0)
    top = r < 4
    return [jnp.where(r < 5, a, b5),
            jnp.where(top, a, jnp.where(r == 4, b, c5)),
            jnp.where(top, a, jnp.where(r == 4, c, b5))]


def dot_tiles(L, scale, first):
    r = rows8()
    t = jnp.where(r < 3, L * scale, 0.0)
    a, b, _ = split3(t)
    a4, b4 = pltpu.roll(a, 4, 0), pltpu.roll(b, 4, 0)
    if first:
        return [a + a4, b + b4]
    return [a + b4, a + b4]


def load(ref, idx):
    dev = idx // 2
    h = idx % 2
    P = ref[dev, :, pl.ds(pl.multiple_of(h * CS, CS), CS)]
    ci = ref[dev, :, 1024:1152]
    ci = jnp.where(h == 1, pltpu.roll(ci, 4, 0), ci)
    return P, jnp.concatenate([ci[t:t + 1] for t in range(4)], 1)


def kernel(first_s, second_s, kind_s, row_ref, col_ref, ro_ref, co_ref, lt, cb, accd, accm, rhs):
    accm[...] = jnp.zeros_like(accm)
    zt = jnp.zeros((8, CS), f32)

    def prep(I, _):
        P, ci = load(row_ref, I)
        L = pltpu.roll(P, 4, 0)
        tiles = (dist_tiles(P, L, 0, True) + dist_tiles(P, L, 1.0, True)
                 + dist_tiles(P, L, -1.0, True) + dot_tiles(L, 0.25, True))
        r = rows8()
        cur = jnp.where(r == 0, P[7:8], jnp.where(r == 1, ci, 0.0))
        a, b, c = split3(cur)
        tiles += [a, b, c, zt, zt]
        full = jnp.concatenate(tiles, 0)
        T = full.T.astype(bf16)
        lt[I] = T
        sel = lax.broadcasted_iota(jnp.int32, (128, 256), 0)
        ln = lax.broadcasted_iota(jnp.int32, (128, 256), 1)
        ones = jnp.where((sel >= 88) & (sel < 112) & (sel % 8 == ln // 128), 1.0, 0.0).astype(bf16)
        o = jnp.dot(T, ones, preferred_element_type=f32)
        cb[I] = o
        accd[I] = jnp.zeros((CS, 256), f32)
        return 0

    lax.fori_loop(0, 16, prep, 0)

    def slot(k, _):
        I = first_s[k]
        J = second_s[k]
        kind = kind_s[k]

        def work(near):
            P, ci = load(col_ref, J)
            cr = P[7:8]
            L = pltpu.roll(P, 4, 0)
            if near:
                vp = dist_tiles(P, L, 1.0, False)
                vm = dist_tiles(P, L, -1.0, False)
                z3 = [zt] * 3
                mats = [z3 + vp + z3, z3 + vm + z3, z3 + z3 + vp, z3 + z3 + vm]
                mats = [m + [zt] * 7 for m in mats]
                mats += [[zt] * 9 + dot_tiles(L, 0.25, False) + [zt] * 5]
            else:
                mats = [dist_tiles(P, L, 0, False) + [zt] * 13,
                        [zt] * 9 + dot_tiles(L, 1.0, False) + [zt] * 5]
            R = [jnp.concatenate(m, 0).astype(bf16) for m in mats]
            mr = [[None] * 4, [None] * 4]
            crs = [jnp.broadcast_to(cr[:, 128 * t:128 * t + 128], (8, 128)) for t in range(4)]
            cis = [jnp.broadcast_to(ci[:, 128 * t:128 * t + 128], (8, 128)) for t in range(4)]
            for m in range(0, CS, M):
                lhs = lt[I, m:m + M, :]
                o = [jnp.dot(lhs, x, preferred_element_type=f32) for x in R]
                for q in range(0, M, 8):
                    bc = cb[I, m + q:m + q + 8, :]
                    br, bi = bc[:, :128], bc[:, 128:]
                    dr = di = None
                    for t in range(4):
                        ri = None
                        for x in o[:-1]:
                            v = lax.rsqrt(x[q:q + 8, 128 * t:128 * t + 128])
                            ri = v if ri is None else ri + v
                        g = ri * o[-1][q:q + 8, 128 * t:128 * t + 128]
                        a, b = g * crs[t], g * cis[t]
                        dr = a if dr is None else dr + a
                        di = b if di is None else di + b
                        a, b = g * br, g * bi
                        mr[0][t] = a if mr[0][t] is None else mr[0][t] + a
                        mr[1][t] = b if mr[1][t] is None else mr[1][t] + b
                    accd[I, m + q:m + q + 8, 0:128] += dr
                    accd[I, m + q:m + q + 8, 128:256] += di
            w = jnp.where(kind >= 4, 0.0, 1.0)
            for c in range(2):
                accm[J, c] += w * jnp.concatenate(mr[c], 1)

        @pl.when((kind & 3) == 1)
        def _():
            work(False)

        @pl.when((kind & 3) == 2)
        def _():
            work(True)
        return 0

    lax.fori_loop(0, 32, slot, 0)

    def fin_row(i, _):
        for h in range(2):
            x = accd[2 * i + h]
            hi = x.astype(bf16)
            lo = (x - hi.astype(f32)).astype(bf16)
            one = jnp.ones((8, 128), bf16)
            for c in range(2):
                s = lax.dot_general(one, hi[:, 128 * c:128 * c + 128], NT, preferred_element_type=f32)
                s = s + lax.dot_general(one, lo[:, 128 * c:128 * c + 128], NT, preferred_element_type=f32)
                ro_ref[i, c:c + 1, h * CS:(h + 1) * CS] = s[0:1]
        return 0
    lax.fori_loop(0, 8, fin_row, 0)

    def fin_col(i, _):
        for h in range(2):
            for c in range(2):
                co_ref[i, c:c + 1, h * CS:(h + 1) * CS] = jnp.sum(accm[2 * i + h, c], 0, keepdims=True)
        return 0
    lax.fori_loop(0, 16, fin_col, 0)


def pre_kernel(pos_ref, seg_ref, rad_ref, cur_ref, slot_ref, out_ref):
    q = pos_ref[...] - 0.5
    a = rad_ref[...]
    n = (q[0:1] * q[0:1] + q[1:2] * q[1:2]) + (q[2:3] * q[2:3] + a * a)
    A = jnp.concatenate([q, n, seg_ref[...], cur_ref[0:1]], 0)
    B = cur_ref[1:2]
    a0, a1, a2 = split3(A)
    b0, b1, b2 = split3(B)
    X = jnp.concatenate([a0, a1, a2, b0, b1, b2, jnp.zeros((5, 1024), f32)], 0).astype(bf16)
    S = jnp.broadcast_to(slot_ref[...].astype(f32), (128, 1024)).T
    lane = lax.broadcasted_iota(jnp.int32, (1024, 128), 1).astype(f32)
    for g in range(0, 8, 2):
        hot = jnp.concatenate([jnp.where(S == lane + 128.0 * (g + i), 1.0, 0.0) for i in range(2)], 1)
        o = jnp.dot(X, hot.astype(bf16), preferred_element_type=f32)
        out_ref[:, 128 * g:128 * g + 256] = o[0:8] + o[8:16] + o[16:24]
        b = o[24:25] + o[25:26] + o[26:27]
        out_ref[g:g + 1, 1024:1152] = b[:, 0:128]
        out_ref[g + 1:g + 2, 1024:1152] = b[:, 128:256]


def post_kernel(a_ref, b_ref, slot_ref, res_ref, cur_ref, out_ref):
    s = a_ref[0]
    for i in range(1, 8):
        s = s + a_ref[i]
    for i in range(16):
        s = s + b_ref[i]
    p = jnp.concatenate([*split3(s), jnp.zeros((10, 1024), f32)], 0).astype(bf16)
    row = lax.broadcasted_iota(jnp.int32, (1024, 256), 0)
    for g in range(4):
        e = slice(256 * g, 256 * g + 256)
        hot = jnp.where(row == slot_ref[:, e], 1.0, 0.0).astype(bf16)
        o = jnp.dot(p, hot, preferred_element_type=f32)
        o = o[0:2] + o[2:4] + o[4:6]
        r = res_ref[:, e]
        out_ref[0:1, e] = r * cur_ref[0:1, e] - o[1:2]
        out_ref[1:2, e] = r * cur_ref[1:2, e] + o[0:1]


def spread(value, axis):
    copies = jnp.broadcast_to(value, (lax.axis_size(axis), *value.shape))
    return lax.all_to_all(copies, axis, 0, 0, tiled=True)


SM = pl.BlockSpec(memory_space=pltpu.SMEM)
VM = pl.BlockSpec(memory_space=pltpu.VMEM)
PARAMS = pltpu.CompilerParams(vmem_limit_bytes=48 << 20)


def on_device(positions, segments, radius, currents, resist, slot_of, pair_list, near_flag):
    slot = slot_of.reshape(1, 1024)
    block = pl.pallas_call(
        pre_kernel, out_shape=jax.ShapeDtypeStruct((8, 1152), f32),
        in_specs=[VM] * 5, out_specs=VM, compiler_params=PARAMS, name="pre",
    )(positions, segments, radius.reshape(1, 1024), currents, slot)
    row = spread(block, "col")
    col = spread(block, "row")
    first = pair_list[:, 0] % 16
    second = pair_list[:, 1] // 16 * 2 + pair_list[:, 1] % 2
    kind = near_flag + jnp.where(pair_list[:, 0] == pair_list[:, 1], 4, 0)
    ro, co = pl.pallas_call(
        kernel,
        out_shape=(jax.ShapeDtypeStruct((8, 2, 1024), f32), jax.ShapeDtypeStruct((16, 2, 1024), f32)),
        in_specs=[SM, SM, SM, VM, VM], out_specs=(VM, VM),
        scratch_shapes=[pltpu.VMEM((16, CS, 128), bf16), pltpu.VMEM((16, CS, 256), f32),
                        pltpu.VMEM((16, CS, 256), f32), pltpu.VMEM((32, 2, 8, CS), f32),
                        pltpu.VMEM((8, 128), f32)],
        compiler_params=PARAMS, name="pairs",
    )(first, second, kind, row, col)
    a = lax.all_to_all(ro, "col", 0, 0, tiled=True)
    b = lax.all_to_all(co, "row", 0, 0, tiled=True)
    return pl.pallas_call(
        post_kernel, out_shape=jax.ShapeDtypeStruct((2, 1024), f32),
        in_specs=[VM] * 5, out_specs=VM, compiler_params=PARAMS, name="post",
    )(a, b, slot, resist.reshape(1, 1024), currents)


def solution(mesh):
    both = ("row", "col")
    return jax.shard_map(
        on_device, mesh=mesh,
        in_specs=(P_(None, both), P_(None, both), P_(both), P_(None, both), P_(both), P_(both),
                  P_(both, None), P_(both)),
        out_specs=P_(None, both), check_vma=False,
    )
```

```python
import math
import jax
import jax.numpy as jnp
from jax import lax
from jax.experimental import pallas as pl
from jax.experimental.pallas import tpu as pltpu
from jax.sharding import PartitionSpec as P_

CS = 512
G = 0.5 / math.sqrt(3.0)
f32, bf16 = jnp.float32, jnp.bfloat16
M = 256
FAR_UNROLL = 2


def split3(x):
    a = x.astype(bf16).astype(f32)
    r = x - a
    b = r.astype(bf16).astype(f32)
    return a, b, r - b


def rows8():
    return lax.broadcasted_iota(jnp.int32, (8, CS), 0)


def moved(P, L, s):
    if s == 0:
        return P, P[3:4]
    w = (G * L) * (2.0 * s * P + G * L)
    n = P[3:4] + ((w[0:1] + w[1:2]) + w[2:3])
    return P + (s * G) * L, n


def dist_tiles(P, L, s, first):
    Q, n = moved(P, L, s)
    r = rows8()
    if first:
        t = jnp.where(r < 3, -2.0 * Q, jnp.where(r == 3, n, jnp.where(r == 4, 1.0, 0.0)))
    else:
        t = jnp.where(r < 3, Q, jnp.where(r == 3, 1.0, jnp.where(r == 4, n, 0.0)))
    a, b, c = split3(t)
    if first:
        b = jnp.where(r == 4, 1.0, b)
        c = jnp.where(r == 4, 1.0, c)
        a5, b5 = pltpu.roll(a, 5, 0), pltpu.roll(b, 5, 0)
        return [jnp.where(r < 5, a, a5), jnp.where(r < 5, b, a5), jnp.where(r < 5, c, b5)]
    a5, b5, c5 = pltpu.roll(a, 5, 0), pltpu.roll(b, 5, 0), pltpu.roll(c, 5, 0)
    return [jnp.where(r < 5, a, b5),
            jnp.where(r < 4, a, jnp.where(r == 4, b, c5)),
            jnp.where(r < 4, a, jnp.where(r == 4, c, b5))]


def dot_tiles(L, scale, first):
    t = jnp.where(rows8() < 3, L * scale, 0.0)
    a, b, c = split3(t)
    a4, b4, c4 = (pltpu.roll(x, 4, 0) for x in (a, b, c))
    if first:
        return [a + a4, b + b4, a + c4]
    return [a + b4, a + b4, c + a4]


def load(ref, idx):
    dev = idx // 2
    h = idx % 2
    P = ref[dev, :, pl.ds(pl.multiple_of(h * CS, CS), CS)]
    ci = ref[dev, :, 1024:1152]
    ci = jnp.where(h == 1, pltpu.roll(ci, 4, 0), ci)
    return P, jnp.concatenate([ci[t:t + 1] for t in range(4)], 1)


def prep_kernel(row_ref, lt):
    zt = jnp.zeros((8, CS), f32)

    def prep(I, _):
        P, ci = load(row_ref, I)
        L = pltpu.roll(P, 4, 0)
        r = rows8()
        cur = jnp.where(r == 0, P[7:8], jnp.where(r == 1, ci, 0.0))
        tiles = (dist_tiles(P, L, 0, True) + [zt] + dist_tiles(P, L, 1.0, True) + [zt]
                 + dist_tiles(P, L, -1.0, True) + [zt] + dot_tiles(L, 0.25, True) + [cur])
        lt[I] = jnp.concatenate(tiles, 0).T
        return 0

    lax.fori_loop(0, 16, prep, 0)


def kernel(pair_s, flag_s, lt_hbm, col_ref, r0, r1, r2, r3, c0, c1, c2, c3, accd, accm, far_s, near_s,
           lt, sem):
    fetch = pltpu.make_async_copy(lt_hbm, lt, sem)
    fetch.start()
    accm[...] = jnp.zeros_like(accm)
    zt = jnp.zeros((8, CS), f32)

    def clear(i, _):
        accd[i] = jnp.zeros((CS, 256), f32)
        return 0
    lax.fori_loop(0, 16, clear, 0)

    fetch.wait()
    me_row, me_col = pair_s[0, 0] // 16, pair_s[0, 1] // 2 % 8

    def sort(k, c):
        nf, nn = c
        I, J, fl = pair_s[k, 0], pair_s[k, 1], flag_s[k]
        code = (I % 16) ^ (2 * me_col)
        code = code + (J // 16 * 2 + J % 2) * 16 + 512
        code = jnp.where(I == J, code, code + 1024)
        far_s[nf] = code
        near_s[nn] = code
        return nf + (fl == 1).astype(jnp.int32), nn + (fl == 2).astype(jnp.int32)
    nf, nn = lax.fori_loop(0, 32, sort, (0, 0))
    for u in range(FAR_UNROLL):
        far_s[nf + u] = 0

    def open_pair(code, near):
        I, J = code % 16, code // 16 % 32
        wd = jnp.where((code // 512) % 2 == 1, 1.0, 0.0)
        wm = jnp.where(code // 1024 == 1, 1.0, 0.0)
        P, ci = load(col_ref, J)
        cr = P[7:8]
        L = pltpu.roll(P, 4, 0)
        z4 = [zt] * 4
        if near:
            vp = dist_tiles(P, L, 1.0, False) + [zt]
            vm = dist_tiles(P, L, -1.0, False) + [zt]
            mats = [z4 + vp + z4 + z4, z4 + z4 + vm + z4, z4 + vm + z4 + z4, z4 + z4 + vp + z4,
                    z4 * 3 + dot_tiles(L, 0.25, False) + [zt]]
            gain = 1.0
        else:
            mats = [dist_tiles(P, L, 0, False) + [zt] + z4 * 3,
                    z4 * 3 + dot_tiles(L, 1.0, False) + [zt]]
            gain = 1.0
        R = [jnp.concatenate(m, 0).astype(bf16) for m in mats]
        crs = [jnp.broadcast_to(cr[:, 128 * t:128 * t + 128] * (wd * gain), (8, 128)) for t in range(4)]
        cis = [jnp.broadcast_to(ci[:, 128 * t:128 * t + 128] * (wd * gain), (8, 128)) for t in range(4)]
        return dict(I=I, J=J, w=wm * gain, R=R, crs=crs, cis=cis, mr=[[None] * 4, [None] * 4])

    def advance(p, m, near):
        I, mr = p["I"], p["mr"]
        lhs = lt[I, m:m + M, :].astype(bf16)
        o = [jnp.dot(lhs, x, preferred_element_type=f32) for x in p["R"]]
        for q in range(0, M, 8):
            bc = lt[I, m + q:m + q + 8, :]
            br = jnp.broadcast_to(bc[:, 120:121], (8, 128))
            bi = jnp.broadcast_to(bc[:, 121:122], (8, 128))
            dr = di = None
            for t in range(4):
                x = [y[q:q + 8, 128 * t:128 * t + 128] for y in o]
                if near:
                    ri = (lax.rsqrt(x[0]) + lax.rsqrt(x[1])) + (lax.rsqrt(x[2]) + lax.rsqrt(x[3]))
                else:
                    ri = lax.rsqrt(x[0])
                g = ri * x[-1]
                a, b = g * p["crs"][t], g * p["cis"][t]
                dr = a if dr is None else dr + a
                di = b if di is None else di + b
                a, b = g * br, g * bi
                mr[0][t] = a if mr[0][t] is None else mr[0][t] + a
                mr[1][t] = b if mr[1][t] is None else mr[1][t] + b
            accd[I, m + q:m + q + 8, 0:128] += dr
            accd[I, m + q:m + q + 8, 128:256] += di

    def close_pair(p):
        for c in range(2):
            accm[p["J"], c] += p["w"] * jnp.concatenate(p["mr"][c], 1)

    def near_step(k, _):
        p = open_pair(near_s[k], True)
        for m in range(0, CS, M):
            advance(p, m, True)
        close_pair(p)
        return 0
    lax.fori_loop(0, nn, near_step, 0)

    def far_step(k, _):
        ps = [open_pair(far_s[FAR_UNROLL * k + u], False) for u in range(FAR_UNROLL)]
        for m in range(0, CS, M):
            for p in ps:
                advance(p, m, False)
        for p in ps:
            close_pair(p)
        return 0
    lax.fori_loop(0, (nf + FAR_UNROLL - 1) // FAR_UNROLL, far_step, 0)

    sel = lax.broadcasted_iota(jnp.int32, (256, 128), 0)
    ln = lax.broadcasted_iota(jnp.int32, (256, 128), 1)
    ones = jnp.where(sel // 128 == ln, 1.0, 0.0).astype(bf16)

    def fin_row(out, m):
        def step(i, _):
            for h in range(2):
                x = accd[4 * m + 2 * i + h]
                hi = x.astype(bf16)
                lo = (x - hi.astype(f32)).astype(bf16)
                s = (jnp.dot(hi, ones, preferred_element_type=f32)
                     + jnp.dot(lo, ones, preferred_element_type=f32))
                out[i, :, h * CS:(h + 1) * CS] = s.T[0:2]
            return 0
        lax.fori_loop(0, 2, step, 0)
    for m, out in enumerate((r0, r1, r2, r3)):
        fin_row(out, m)

    for m, out in enumerate((c0, c1, c2, c3)):
        for k in range(4):
            slot = k // 2 * 8 + 2 * m + k % 2
            src = 2 * jnp.bitwise_xor(slot, me_row)
            for h in range(2):
                for c in range(2):
                    out[k, c:c + 1, h * CS:(h + 1) * CS] = jnp.sum(accm[src + h, c], 0, keepdims=True)


SCRATCH = [pltpu.VMEM((16, CS, 256), f32), pltpu.VMEM((32, 2, 8, CS), f32),
           pltpu.SMEM((40,), jnp.int32), pltpu.SMEM((40,), jnp.int32),
           pltpu.VMEM((16, CS, 128), f32), pltpu.SemaphoreType.DMA]


def pre_kernel(pos_hbm, seg_hbm, rad_hbm, cur_hbm, slot_hbm, one_ref, all_ref,
               pos_ref, seg_ref, rad_ref, cur_ref, slot_ref, sems):
    moves = [pltpu.make_async_copy(a, b, sems.at[i]) for i, (a, b) in enumerate(
        ((pos_hbm, pos_ref), (seg_hbm, seg_ref), (rad_hbm, rad_ref), (cur_hbm, cur_ref),
         (slot_hbm, slot_ref)))]
    out_ref = one_ref.at[0]
    for move in moves:
        move.start()
    for move in moves:
        move.wait()
    q = pos_ref[...] - 0.5
    a = rad_ref[...]
    n = (q[0:1] * q[0:1] + q[1:2] * q[1:2]) + (q[2:3] * q[2:3] + a * a)
    A = jnp.concatenate([q, n, seg_ref[...], cur_ref[0:1]], 0)
    B = cur_ref[1:2]
    a0, a1, a2 = split3(A)
    b0, b1, b2 = split3(B)
    X = jnp.concatenate([a0, a1, a2, b0, b1, b2, jnp.zeros((5, 1024), f32)], 0).astype(bf16)
    S = jnp.broadcast_to(slot_ref[...].astype(f32), (128, 1024)).T
    lane = lax.broadcasted_iota(jnp.int32, (1024, 128), 1).astype(f32)
    for g in range(0, 8, 2):
        hot = jnp.concatenate([jnp.where(S == lane + 128.0 * (g + i), 1.0, 0.0) for i in range(2)], 1)
        o = jnp.dot(X, hot.astype(bf16), preferred_element_type=f32)
        out_ref[:, 128 * g:128 * g + 256] = o[0:8] + o[8:16] + o[16:24]
        b = o[24:25] + o[25:26] + o[26:27]
        out_ref[g:g + 1, 1024:1152] = b[:, 0:128]
        out_ref[g + 1:g + 2, 1024:1152] = b[:, 128:256]
    for i in range(16):
        all_ref[i] = out_ref[...]


def post_kernel(a_ref, b_ref, c_ref, d_ref, slot_ref, res_ref, cur_ref, out_ref):
    s = (a_ref[0] + b_ref[0]) + (c_ref[0] + d_ref[0])
    p = jnp.concatenate([*split3(s), jnp.zeros((10, 1024), f32)], 0).astype(bf16)
    row = lax.broadcasted_iota(jnp.int32, (1024, 256), 0)
    for g in range(4):
        e = slice(256 * g, 256 * g + 256)
        hot = jnp.where(row == slot_ref[:, e], 1.0, 0.0).astype(bf16)
        o = jnp.dot(p, hot, preferred_element_type=f32)
        o = o[0:2] + o[2:4] + o[4:6]
        r = res_ref[:, e]
        out_ref[0:1, e] = r * cur_ref[0:1, e] - o[1:2]
        out_ref[1:2, e] = r * cur_ref[1:2, e] + o[0:1]


SM = pl.BlockSpec(memory_space=pltpu.SMEM)
VM = pl.BlockSpec(memory_space=pltpu.VMEM)
HB = pl.BlockSpec(memory_space=pltpu.HBM)
BIG = pltpu.CompilerParams(vmem_limit_bytes=61 << 20)
PARAMS = pltpu.CompilerParams(vmem_limit_bytes=24 << 20)


def shape(*dims):
    return jax.ShapeDtypeStruct(dims, f32)


def swap(value, axis, k):
    return lax.ppermute(value, axis, [(i, i ^ k) for i in range(lax.axis_size(axis))])


def on_device(positions, segments, radius, currents, resist, slot_of, pair_list, near_flag):
    slot = slot_of.reshape(1, 1024)
    block, copies = pl.pallas_call(
        pre_kernel, out_shape=(shape(1, 8, 1152), shape(16, 8, 1152)),
        in_specs=[HB] * 5, out_specs=(VM, VM),
        scratch_shapes=[pltpu.VMEM((3, 1024), f32), pltpu.VMEM((3, 1024), f32),
                        pltpu.VMEM((1, 1024), f32), pltpu.VMEM((2, 1024), f32),
                        pltpu.VMEM((1, 1024), jnp.int32), pltpu.SemaphoreType.DMA((5,))],
        compiler_params=pltpu.CompilerParams(vmem_limit_bytes=62 << 20), name="pre",
    )(positions, segments, radius.reshape(1, 1024), currents, slot)
    col = lax.all_to_all(copies, "row", 0, 0, tiled=True)
    two = jnp.concatenate([block, swap(block, "col", 1)], 0)
    row = jnp.concatenate([two] + [swap(two, "col", 2 * m) for m in (1, 2, 3)], 0)
    lt = pl.pallas_call(
        prep_kernel, out_shape=shape(16, CS, 128), in_specs=[VM], out_specs=VM,
        compiler_params=BIG, name="prep",
        cost_estimate=pl.CostEstimate(flops=10**9, bytes_accessed=5 << 20, transcendentals=0),
    )(row)
    outs = pl.pallas_call(
        kernel, out_shape=(shape(2, 2, 1024),) * 4 + (shape(4, 2, 1024),) * 4,
        in_specs=[SM, SM, HB, VM], out_specs=(VM,) * 8, scratch_shapes=SCRATCH,
        compiler_params=BIG, name="pairs",
    )(pair_list, near_flag, lt, col)
    a, b = outs[:4], outs[4:]
    b = [b[0]] + [swap(b[m], "row", 2 * m) for m in (1, 2, 3)]
    a = [a[0]] + [swap(a[m], "col", 2 * m) for m in (1, 2, 3)]
    b = (b[0] + b[1]) + (b[2] + b[3])
    a = (a[0] + a[1]) + (a[2] + a[3])
    b = b[0:2] + swap(b[2:4], "row", 8)
    parts = (a[0:1], swap(a[1:2], "col", 1), b[0:1], swap(b[1:2], "row", 1))
    return pl.pallas_call(
        post_kernel, out_shape=shape(2, 1024), in_specs=[VM] * 7, out_specs=VM,
        compiler_params=PARAMS, name="post",
    )(*parts, slot, resist.reshape(1, 1024), currents)


def solution(mesh):
    both = ("row", "col")
    return jax.shard_map(
        on_device, mesh=mesh,
        in_specs=(P_(None, both), P_(None, both), P_(both), P_(None, both), P_(both), P_(both),
                  P_(both, None), P_(both)),
        out_specs=P_(None, both), check_vma=False,
    )
```

```python
import math
import jax
import jax.numpy as jnp
from jax import lax
from jax.experimental import pallas as pl
from jax.experimental.pallas import tpu as pltpu
from jax.sharding import PartitionSpec as P_

CS = 512
G = 0.5 / math.sqrt(3.0)
f32, bf16 = jnp.float32, jnp.bfloat16
M = 256
FAR_UNROLL = 2


def split3(x):
    a = x.astype(bf16).astype(f32)
    r = x - a
    b = r.astype(bf16).astype(f32)
    return a, b, r - b


def rows8():
    return lax.broadcasted_iota(jnp.int32, (8, CS), 0)


def moved(P, L, s):
    if s == 0:
        return P, P[3:4]
    w = (G * L) * (2.0 * s * P + G * L)
    n = P[3:4] + ((w[0:1] + w[1:2]) + w[2:3])
    return P + (s * G) * L, n


def dist_tiles(P, L, s, first):
    Q, n = moved(P, L, s)
    r = rows8()
    if first:
        t = jnp.where(r < 3, -2.0 * Q, jnp.where(r == 3, n, jnp.where(r == 4, 1.0, 0.0)))
    else:
        t = jnp.where(r < 3, Q, jnp.where(r == 3, 1.0, jnp.where(r == 4, n, 0.0)))
    a, b, c = split3(t)
    if first:
        b = jnp.where(r == 4, 1.0, b)
        c = jnp.where(r == 4, 1.0, c)
        a5, b5 = pltpu.roll(a, 5, 0), pltpu.roll(b, 5, 0)
        return [jnp.where(r < 5, a, a5), jnp.where(r < 5, b, a5), jnp.where(r < 5, c, b5)]
    a5, b5, c5 = pltpu.roll(a, 5, 0), pltpu.roll(b, 5, 0), pltpu.roll(c, 5, 0)
    return [jnp.where(r < 5, a, b5),
            jnp.where(r < 4, a, jnp.where(r == 4, b, c5)),
            jnp.where(r < 4, a, jnp.where(r == 4, c, b5))]


def dot_tiles(L, scale, first):
    t = jnp.where(rows8() < 3, L * scale, 0.0)
    a, b, c = split3(t)
    a4, b4, c4 = (pltpu.roll(x, 4, 0) for x in (a, b, c))
    if first:
        return [a + a4, b + b4, a + c4]
    return [a + b4, a + b4, c + a4]


def load(ref, idx):
    dev = idx // 2
    h = idx % 2
    P = ref[dev, :, pl.ds(pl.multiple_of(h * CS, CS), CS)]
    ci = ref[dev, :, 1024:1152]
    ci = jnp.where(h == 1, pltpu.roll(ci, 4, 0), ci)
    return P, jnp.concatenate([ci[t:t + 1] for t in range(4)], 1)


def prep(ref, m, lt):
    zt = jnp.zeros((8, CS), f32)

    def step(i, _):
        for h in range(2):
            P = ref[i, :, CS * h:CS * h + CS]
            ci = ref[i, :, 1024:1152]
            ci = jnp.concatenate([ci[4 * h + t:4 * h + t + 1] for t in range(4)], 1)
            L = pltpu.roll(P, 4, 0)
            r = rows8()
            cur = jnp.where(r == 0, P[7:8], jnp.where(r == 1, ci, 0.0))
            tiles = (dist_tiles(P, L, 0, True) + [zt] + dist_tiles(P, L, 1.0, True) + [zt]
                     + dist_tiles(P, L, -1.0, True) + [zt] + dot_tiles(L, 0.25, True) + [cur])
            lt[4 * m + 2 * i + h] = jnp.concatenate(tiles, 0).T
        return 0

    lax.fori_loop(0, 2, step, 0)


def kernel(pair_s, flag_s, w0, w1, w2, w3, col_ref, r0, r1, r2, r3, c0, c1, c2, c3,
           accd, accm, far_s, near_s, lt):
    for m, ref in enumerate((w0, w1, w2, w3)):
        prep(ref, m, lt)
    accm[...] = jnp.zeros_like(accm)
    zt = jnp.zeros((8, CS), f32)

    def clear(i, _):
        accd[i] = jnp.zeros((CS, 256), f32)
        return 0
    lax.fori_loop(0, 16, clear, 0)

    me_row, me_col = pair_s[0, 0] // 16, pair_s[1, 0] // 2 % 8

    def sort(k, c):
        nf, nn = c
        I, J, fl = pair_s[0, k], pair_s[1, k], flag_s[k]
        code = (I % 16) ^ (2 * me_col)
        code = code + (J // 16 * 2 + J % 2) * 16 + 512
        code = jnp.where(I == J, code, code + 1024)
        far_s[nf] = code
        near_s[nn] = code
        return nf + (fl == 1).astype(jnp.int32), nn + (fl == 2).astype(jnp.int32)
    nf, nn = lax.fori_loop(0, 32, sort, (0, 0))
    for u in range(FAR_UNROLL):
        far_s[nf + u] = 0

    def open_pair(code, near):
        I, J = code % 16, code // 16 % 32
        wd = jnp.where((code // 512) % 2 == 1, 1.0, 0.0)
        wm = jnp.where(code // 1024 == 1, 1.0, 0.0)
        P, ci = load(col_ref, J)
        cr = P[7:8]
        L = pltpu.roll(P, 4, 0)
        z4 = [zt] * 4
        if near:
            vp = dist_tiles(P, L, 1.0, False) + [zt]
            vm = dist_tiles(P, L, -1.0, False) + [zt]
            mats = [z4 + vp + z4 + z4, z4 + z4 + vm + z4, z4 + vm + z4 + z4, z4 + z4 + vp + z4,
                    z4 * 3 + dot_tiles(L, 0.25, False) + [zt]]
            gain = 1.0
        else:
            mats = [dist_tiles(P, L, 0, False) + [zt] + z4 * 3,
                    z4 * 3 + dot_tiles(L, 1.0, False) + [zt]]
            gain = 1.0
        R = [jnp.concatenate(m, 0).astype(bf16) for m in mats]
        crs = [jnp.broadcast_to(cr[:, 128 * t:128 * t + 128] * (wd * gain), (8, 128)) for t in range(4)]
        cis = [jnp.broadcast_to(ci[:, 128 * t:128 * t + 128] * (wd * gain), (8, 128)) for t in range(4)]
        return dict(I=I, J=J, w=wm * gain, R=R, crs=crs, cis=cis, mr=[[None] * 4, [None] * 4])

    def advance(p, m, near):
        I, mr = p["I"], p["mr"]
        lhs = lt[I, m:m + M, :].astype(bf16)
        o = [jnp.dot(lhs, x, preferred_element_type=f32) for x in p["R"]]
        for q in range(0, M, 8):
            bc = lt[I, m + q:m + q + 8, :]
            br = jnp.broadcast_to(bc[:, 120:121], (8, 128))
            bi = jnp.broadcast_to(bc[:, 121:122], (8, 128))
            dr = di = None
            for t in range(4):
                x = [y[q:q + 8, 128 * t:128 * t + 128] for y in o]
                if near:
                    ri = (lax.rsqrt(x[0]) + lax.rsqrt(x[1])) + (lax.rsqrt(x[2]) + lax.rsqrt(x[3]))
                else:
                    ri = lax.rsqrt(x[0])
                g = ri * x[-1]
                a, b = g * p["crs"][t], g * p["cis"][t]
                dr = a if dr is None else dr + a
                di = b if di is None else di + b
                a, b = g * br, g * bi
                mr[0][t] = a if mr[0][t] is None else mr[0][t] + a
                mr[1][t] = b if mr[1][t] is None else mr[1][t] + b
            accd[I, m + q:m + q + 8, 0:128] += dr
            accd[I, m + q:m + q + 8, 128:256] += di

    def close_pair(p):
        for c in range(2):
            accm[p["J"], c] += p["w"] * jnp.concatenate(p["mr"][c], 1)

    def near_step(k, _):
        p = open_pair(near_s[k], True)
        for m in range(0, CS, M):
            advance(p, m, True)
        close_pair(p)
        return 0
    lax.fori_loop(0, nn, near_step, 0)

    def far_step(k, _):
        ps = [open_pair(far_s[FAR_UNROLL * k + u], False) for u in range(FAR_UNROLL)]
        for m in range(0, CS, M):
            for p in ps:
                advance(p, m, False)
        for p in ps:
            close_pair(p)
        return 0
    lax.fori_loop(0, (nf + FAR_UNROLL - 1) // FAR_UNROLL, far_step, 0)

    sel = lax.broadcasted_iota(jnp.int32, (256, 128), 0)
    ln = lax.broadcasted_iota(jnp.int32, (256, 128), 1)
    ones = jnp.where(sel // 128 == ln, 1.0, 0.0).astype(bf16)

    def fin_row(out, m):
        def step(i, _):
            for h in range(2):
                x = accd[4 * m + 2 * i + h]
                hi = x.astype(bf16)
                lo = (x - hi.astype(f32)).astype(bf16)
                s = (jnp.dot(hi, ones, preferred_element_type=f32)
                     + jnp.dot(lo, ones, preferred_element_type=f32))
                out[i, :, h * CS:(h + 1) * CS] = s.T[0:2]
            return 0
        lax.fori_loop(0, 2, step, 0)
    for m, out in enumerate((r0, r1, r2, r3)):
        fin_row(out, m)

    for m, out in enumerate((c0, c1, c2, c3)):
        for k in range(4):
            slot = k // 2 * 8 + 2 * m + k % 2
            src = 2 * jnp.bitwise_xor(slot, me_row)
            for h in range(2):
                for c in range(2):
                    out[k, c:c + 1, h * CS:(h + 1) * CS] = jnp.sum(accm[src + h, c], 0, keepdims=True)


SCRATCH = [pltpu.VMEM((16, CS, 256), f32), pltpu.VMEM((32, 2, 8, CS), f32),
           pltpu.SMEM((40,), jnp.int32), pltpu.SMEM((40,), jnp.int32),
           pltpu.VMEM((16, CS, 128), f32)]


def pre_kernel(pos_hbm, seg_hbm, rad_hbm, cur_hbm, slot_hbm, one_ref, all_ref,
               pos_ref, seg_ref, rad_ref, cur_ref, slot_ref, sems):
    moves = [pltpu.make_async_copy(a, b, sems.at[i]) for i, (a, b) in enumerate(
        ((pos_hbm, pos_ref), (seg_hbm, seg_ref), (rad_hbm, rad_ref), (cur_hbm, cur_ref),
         (slot_hbm, slot_ref)))]
    out_ref = one_ref.at[0]
    for move in moves:
        move.start()
    for move in moves:
        move.wait()
    q = pos_ref[...] - 0.5
    a = rad_ref[...]
    n = (q[0:1] * q[0:1] + q[1:2] * q[1:2]) + (q[2:3] * q[2:3] + a * a)
    A = jnp.concatenate([q, n, seg_ref[...], cur_ref[0:1]], 0)
    B = cur_ref[1:2]
    a0, a1, a2 = split3(A)
    b0, b1, b2 = split3(B)
    X = jnp.concatenate([a0, a1, a2, b0, b1, b2, jnp.zeros((5, 1024), f32)], 0).astype(bf16)
    S = jnp.broadcast_to(slot_ref[...].astype(f32), (128, 1024)).T
    lane = lax.broadcasted_iota(jnp.int32, (1024, 128), 1).astype(f32)
    for g in range(0, 8, 2):
        hot = jnp.concatenate([jnp.where(S == lane + 128.0 * (g + i), 1.0, 0.0) for i in range(2)], 1)
        o = jnp.dot(X, hot.astype(bf16), preferred_element_type=f32)
        out_ref[:, 128 * g:128 * g + 256] = o[0:8] + o[8:16] + o[16:24]
        b = o[24:25] + o[25:26] + o[26:27]
        out_ref[g:g + 1, 1024:1152] = b[:, 0:128]
        out_ref[g + 1:g + 2, 1024:1152] = b[:, 128:256]
    for i in range(16):
        all_ref[i] = out_ref[...]


def post_kernel(a_ref, b_ref, c_ref, d_ref, slot_ref, res_ref, cur_ref, out_ref):
    s = (a_ref[0] + b_ref[0]) + (c_ref[0] + d_ref[0])
    p = jnp.concatenate([*split3(s), jnp.zeros((10, 1024), f32)], 0).astype(bf16)
    row = lax.broadcasted_iota(jnp.int32, (1024, 256), 0)
    for g in range(4):
        e = slice(256 * g, 256 * g + 256)
        hot = jnp.where(row == slot_ref[:, e], 1.0, 0.0).astype(bf16)
        o = jnp.dot(p, hot, preferred_element_type=f32)
        o = o[0:2] + o[2:4] + o[4:6]
        r = res_ref[:, e]
        out_ref[0:1, e] = r * cur_ref[0:1, e] - o[1:2]
        out_ref[1:2, e] = r * cur_ref[1:2, e] + o[0:1]


SM = pl.BlockSpec(memory_space=pltpu.SMEM)
VM = pl.BlockSpec(memory_space=pltpu.VMEM)
HB = pl.BlockSpec(memory_space=pltpu.HBM)
PARAMS = pltpu.CompilerParams(vmem_limit_bytes=24 << 20)


def shape(*dims):
    return jax.ShapeDtypeStruct(dims, f32)


def swap(value, axis, k):
    return lax.ppermute(value, axis, [(i, i ^ k) for i in range(lax.axis_size(axis))])


def on_device(positions, segments, radius, currents, resist, slot_of, pair_list, near_flag):
    slot = slot_of.reshape(1, 1024)
    block, copies = pl.pallas_call(
        pre_kernel, out_shape=(shape(1, 8, 1152), shape(16, 8, 1152)),
        in_specs=[HB] * 5, out_specs=(VM, VM),
        scratch_shapes=[pltpu.VMEM((3, 1024), f32), pltpu.VMEM((3, 1024), f32),
                        pltpu.VMEM((1, 1024), f32), pltpu.VMEM((2, 1024), f32),
                        pltpu.VMEM((1, 1024), jnp.int32), pltpu.SemaphoreType.DMA((5,))],
        compiler_params=pltpu.CompilerParams(vmem_limit_bytes=62 << 20), name="pre",
    )(positions, segments, radius.reshape(1, 1024), currents, slot)
    col = lax.all_to_all(copies, "row", 0, 0, tiled=True)
    two = jnp.concatenate([block, swap(block, "col", 1)], 0)
    row = [two] + [swap(two, "col", 2 * m) for m in (1, 2, 3)]
    outs = pl.pallas_call(
        kernel, out_shape=(shape(2, 2, 1024),) * 4 + (shape(4, 2, 1024),) * 4,
        in_specs=[SM, SM] + [VM] * 5, out_specs=(VM,) * 8, scratch_shapes=SCRATCH,
        compiler_params=PARAMS, name="pairs",
    )(pair_list.T, near_flag, *row, col)
    a, b = outs[:4], outs[4:]
    b = [b[0]] + [swap(b[m], "row", 2 * m) for m in (1, 2, 3)]
    a = [a[0]] + [swap(a[m], "col", 2 * m) for m in (1, 2, 3)]
    b = (b[0] + b[1]) + (b[2] + b[3])
    a = (a[0] + a[1]) + (a[2] + a[3])
    b = b[0:2] + swap(b[2:4], "row", 8)
    parts = (a[0:1], swap(a[1:2], "col", 1), b[0:1], swap(b[1:2], "row", 1))
    return pl.pallas_call(
        post_kernel, out_shape=shape(2, 1024), in_specs=[VM] * 7, out_specs=VM,
        compiler_params=PARAMS, name="post",
    )(*parts, slot, resist.reshape(1, 1024), currents)


def solution(mesh):
    both = ("row", "col")
    return jax.shard_map(
        on_device, mesh=mesh,
        in_specs=(P_(None, both), P_(None, both), P_(both), P_(None, both), P_(both), P_(both),
                  P_(both, None), P_(both)),
        out_specs=P_(None, both), check_vma=False,
    )
```

```python
import math
import jax
import jax.numpy as jnp
from jax import lax
from jax.experimental import pallas as pl
from jax.experimental.pallas import tpu as pltpu
from jax.sharding import PartitionSpec as P_

CS = 512
G = 0.5 / math.sqrt(3.0)
f32, bf16 = jnp.float32, jnp.bfloat16
M = 256
FAR_UNROLL = 2


def split3(x):
    a = x.astype(bf16).astype(f32)
    r = x - a
    b = r.astype(bf16).astype(f32)
    return a, b, r - b


def rows8():
    return lax.broadcasted_iota(jnp.int32, (8, CS), 0)


def moved(P, L, s):
    if s == 0:
        return P, P[3:4]
    w = (G * L) * (2.0 * s * P + G * L)
    n = P[3:4] + ((w[0:1] + w[1:2]) + w[2:3])
    return P + (s * G) * L, n


def dist_tiles(P, L, s, first):
    Q, n = moved(P, L, s)
    r = rows8()
    if first:
        t = jnp.where(r < 3, -2.0 * Q, jnp.where(r == 3, n, jnp.where(r == 4, 1.0, 0.0)))
    else:
        t = jnp.where(r < 3, Q, jnp.where(r == 3, 1.0, jnp.where(r == 4, n, 0.0)))
    a, b, c = split3(t)
    if first:
        b = jnp.where(r == 4, 1.0, b)
        c = jnp.where(r == 4, 1.0, c)
        a5, b5 = pltpu.roll(a, 5, 0), pltpu.roll(b, 5, 0)
        return [jnp.where(r < 5, a, a5), jnp.where(r < 5, b, a5), jnp.where(r < 5, c, b5)]
    a5, b5, c5 = pltpu.roll(a, 5, 0), pltpu.roll(b, 5, 0), pltpu.roll(c, 5, 0)
    return [jnp.where(r < 5, a, b5),
            jnp.where(r < 4, a, jnp.where(r == 4, b, c5)),
            jnp.where(r < 4, a, jnp.where(r == 4, c, b5))]


def dot_tiles(L, scale, first):
    t = jnp.where(rows8() < 3, L * scale, 0.0)
    a, b, c = split3(t)
    a4, b4, c4 = (pltpu.roll(x, 4, 0) for x in (a, b, c))
    if first:
        return [a + a4, b + b4, a + c4]
    return [a + b4, a + b4, c + a4]


def load(ref, idx):
    dev = idx // 2
    h = idx % 2
    P = ref[dev, :, pl.ds(pl.multiple_of(h * CS, CS), CS)]
    ci = ref[dev, :, 1024:1152]
    ci = jnp.where(h == 1, pltpu.roll(ci, 4, 0), ci)
    return P, jnp.concatenate([ci[t:t + 1] for t in range(4)], 1)


def prep(ref, m, lt):
    zt = jnp.zeros((8, CS), f32)

    def step(i, _):
        for h in range(2):
            P = ref[i, :, CS * h:CS * h + CS]
            ci = ref[i, :, 1024:1152]
            ci = jnp.concatenate([ci[4 * h + t:4 * h + t + 1] for t in range(4)], 1)
            L = pltpu.roll(P, 4, 0)
            r = rows8()
            cur = jnp.where(r == 0, P[7:8], jnp.where(r == 1, ci, 0.0))
            tiles = (dist_tiles(P, L, 0, True) + [zt] + dist_tiles(P, L, 1.0, True) + [zt]
                     + dist_tiles(P, L, -1.0, True) + [zt] + dot_tiles(L, 0.25, True) + [cur])
            lt[4 * m + 2 * i + h] = jnp.concatenate(tiles, 0).T
        return 0

    for i in range(2):
        step(i, 0)


def kernel(pair_s, flag_s, w0, w1, w2, w3, col_ref, r0, r1, r2, r3, c0, c1, c2, c3,
           accd, accm, far_s, near_s, lt):
    for m, ref in enumerate((w0, w1, w2, w3)):
        prep(ref, m, lt)
    accm[...] = jnp.zeros_like(accm)
    zt = jnp.zeros((8, CS), f32)

    def clear(i, _):
        accd[i] = jnp.zeros((CS, 256), f32)
        return 0
    lax.fori_loop(0, 16, clear, 0)

    me_row, me_col = pair_s[0, 0] // 16, pair_s[1, 0] // 2 % 8

    def sort(k, c):
        nf, nn = c
        I, J, fl = pair_s[0, k], pair_s[1, k], flag_s[k]
        code = (I % 16) ^ (2 * me_col)
        code = code + (J // 16 * 2 + J % 2) * 16 + 512
        code = jnp.where(I == J, code, code + 1024)
        far_s[nf] = code
        near_s[nn] = code
        return nf + (fl == 1).astype(jnp.int32), nn + (fl == 2).astype(jnp.int32)
    nf, nn = lax.fori_loop(0, 32, sort, (0, 0))
    for u in range(FAR_UNROLL):
        far_s[nf + u] = 0

    def open_pair(code, near):
        I, J = code % 16, code // 16 % 32
        wd = jnp.where((code // 512) % 2 == 1, 1.0, 0.0)
        wm = jnp.where(code // 1024 == 1, 1.0, 0.0)
        P, ci = load(col_ref, J)
        cr = P[7:8]
        L = pltpu.roll(P, 4, 0)
        z4 = [zt] * 4
        if near:
            vp = dist_tiles(P, L, 1.0, False) + [zt]
            vm = dist_tiles(P, L, -1.0, False) + [zt]
            mats = [z4 + vp + z4 + z4, z4 + z4 + vm + z4, z4 + vm + z4 + z4, z4 + z4 + vp + z4,
                    z4 * 3 + dot_tiles(L, 0.25, False) + [zt]]
            gain = 1.0
        else:
            mats = [dist_tiles(P, L, 0, False) + [zt] + z4 * 3,
                    z4 * 3 + dot_tiles(L, 1.0, False) + [zt]]
            gain = 1.0
        R = [jnp.concatenate(m, 0).astype(bf16) for m in mats]
        crs = [jnp.broadcast_to(cr[:, 128 * t:128 * t + 128] * (wd * gain), (8, 128)) for t in range(4)]
        cis = [jnp.broadcast_to(ci[:, 128 * t:128 * t + 128] * (wd * gain), (8, 128)) for t in range(4)]
        return dict(I=I, J=J, w=wm * gain, R=R, crs=crs, cis=cis, mr=[[None] * 4, [None] * 4])

    def advance(p, m, near):
        I, mr = p["I"], p["mr"]
        lhs = lt[I, m:m + M, :].astype(bf16)
        o = [jnp.dot(lhs, x, preferred_element_type=f32) for x in p["R"]]
        for q in range(0, M, 8):
            bc = lt[I, m + q:m + q + 8, :]
            br = jnp.broadcast_to(bc[:, 120:121], (8, 128))
            bi = jnp.broadcast_to(bc[:, 121:122], (8, 128))
            dr = di = None
            for t in range(4):
                x = [y[q:q + 8, 128 * t:128 * t + 128] for y in o]
                if near:
                    ri = (lax.rsqrt(x[0]) + lax.rsqrt(x[1])) + (lax.rsqrt(x[2]) + lax.rsqrt(x[3]))
                else:
                    ri = lax.rsqrt(x[0])
                g = ri * x[-1]
                a, b = g * p["crs"][t], g * p["cis"][t]
                dr = a if dr is None else dr + a
                di = b if di is None else di + b
                a, b = g * br, g * bi
                mr[0][t] = a if mr[0][t] is None else mr[0][t] + a
                mr[1][t] = b if mr[1][t] is None else mr[1][t] + b
            accd[I, m + q:m + q + 8, 0:128] += dr
            accd[I, m + q:m + q + 8, 128:256] += di

    def close_pair(p):
        for c in range(2):
            accm[p["J"], c] += p["w"] * jnp.concatenate(p["mr"][c], 1)

    def near_step(k, _):
        p = open_pair(near_s[k], True)
        for m in range(0, CS, M):
            advance(p, m, True)
        close_pair(p)
        return 0
    lax.fori_loop(0, nn, near_step, 0)

    def far_step(k, _):
        ps = [open_pair(far_s[FAR_UNROLL * k + u], False) for u in range(FAR_UNROLL)]
        for m in range(0, CS, M):
            for p in ps:
                advance(p, m, False)
        for p in ps:
            close_pair(p)
        return 0
    lax.fori_loop(0, (nf + FAR_UNROLL - 1) // FAR_UNROLL, far_step, 0)

    for m, out in enumerate((r0, r1, r2, r3)):
        for i in range(2):
            for h in range(2):
                x = accd[4 * m + 2 * i + h]
                for c in range(2):
                    t = x[:, 128 * c:128 * c + 128].T
                    out[i, c:c + 1, h * CS:(h + 1) * CS] = jnp.sum(t, 0, keepdims=True)

    for m, out in enumerate((c0, c1, c2, c3)):
        for k in range(4):
            slot = k // 2 * 8 + 2 * m + k % 2
            src = 2 * jnp.bitwise_xor(slot, me_row)
            for h in range(2):
                for c in range(2):
                    out[k, c:c + 1, h * CS:(h + 1) * CS] = jnp.sum(accm[src + h, c], 0, keepdims=True)


SCRATCH = [pltpu.VMEM((16, CS, 256), f32), pltpu.VMEM((32, 2, 8, CS), f32),
           pltpu.SMEM((40,), jnp.int32), pltpu.SMEM((40,), jnp.int32),
           pltpu.VMEM((16, CS, 128), f32)]


def pre_kernel(pos_hbm, seg_hbm, rad_hbm, cur_hbm, slot_hbm, one_ref, all_ref,
               pos_ref, seg_ref, rad_ref, cur_ref, slot_ref, sems):
    moves = [pltpu.make_async_copy(a, b, sems.at[i]) for i, (a, b) in enumerate(
        ((pos_hbm, pos_ref), (seg_hbm, seg_ref), (rad_hbm, rad_ref), (cur_hbm, cur_ref),
         (slot_hbm, slot_ref)))]
    out_ref = one_ref.at[0]
    for move in moves:
        move.start()
    for move in moves:
        move.wait()
    q = pos_ref[...] - 0.5
    a = rad_ref[...]
    n = (q[0:1] * q[0:1] + q[1:2] * q[1:2]) + (q[2:3] * q[2:3] + a * a)
    A = jnp.concatenate([q, n, seg_ref[...], cur_ref[0:1]], 0)
    B = cur_ref[1:2]
    a0, a1, a2 = split3(A)
    b0, b1, b2 = split3(B)
    X = jnp.concatenate([a0, a1, a2, b0, b1, b2, jnp.zeros((5, 1024), f32)], 0).astype(bf16)
    S = jnp.broadcast_to(slot_ref[...].astype(f32), (128, 1024)).T
    lane = lax.broadcasted_iota(jnp.int32, (1024, 128), 1).astype(f32)
    for g in range(0, 8, 2):
        hot = jnp.concatenate([jnp.where(S == lane + 128.0 * (g + i), 1.0, 0.0) for i in range(2)], 1)
        o = jnp.dot(X, hot.astype(bf16), preferred_element_type=f32)
        out_ref[:, 128 * g:128 * g + 256] = o[0:8] + o[8:16] + o[16:24]
        b = o[24:25] + o[25:26] + o[26:27]
        out_ref[g:g + 1, 1024:1152] = b[:, 0:128]
        out_ref[g + 1:g + 2, 1024:1152] = b[:, 128:256]
    for i in range(16):
        all_ref[i] = out_ref[...]


def post_kernel(a_ref, b_ref, c_ref, d_ref, slot_ref, res_ref, cur_ref, out_ref):
    s = (a_ref[0] + b_ref[0]) + (c_ref[0] + d_ref[0])
    p = jnp.concatenate([*split3(s), jnp.zeros((10, 1024), f32)], 0).astype(bf16)
    row = lax.broadcasted_iota(jnp.int32, (1024, 256), 0)
    for g in range(4):
        e = slice(256 * g, 256 * g + 256)
        hot = jnp.where(row == slot_ref[:, e], 1.0, 0.0).astype(bf16)
        o = jnp.dot(p, hot, preferred_element_type=f32)
        o = o[0:2] + o[2:4] + o[4:6]
        r = res_ref[:, e]
        out_ref[0:1, e] = r * cur_ref[0:1, e] - o[1:2]
        out_ref[1:2, e] = r * cur_ref[1:2, e] + o[0:1]


SM = pl.BlockSpec(memory_space=pltpu.SMEM)
VM = pl.BlockSpec(memory_space=pltpu.VMEM)
HB = pl.BlockSpec(memory_space=pltpu.HBM)
PARAMS = pltpu.CompilerParams(vmem_limit_bytes=24 << 20)


def shape(*dims):
    return jax.ShapeDtypeStruct(dims, f32)


def swap(value, axis, k):
    return lax.ppermute(value, axis, [(i, i ^ k) for i in range(lax.axis_size(axis))])


def on_device(positions, segments, radius, currents, resist, slot_of, pair_list, near_flag):
    slot = slot_of.reshape(1, 1024)
    block, copies = pl.pallas_call(
        pre_kernel, out_shape=(shape(1, 8, 1152), shape(16, 8, 1152)),
        in_specs=[HB] * 5, out_specs=(VM, VM),
        scratch_shapes=[pltpu.VMEM((3, 1024), f32), pltpu.VMEM((3, 1024), f32),
                        pltpu.VMEM((1, 1024), f32), pltpu.VMEM((2, 1024), f32),
                        pltpu.VMEM((1, 1024), jnp.int32), pltpu.SemaphoreType.DMA((5,))],
        compiler_params=pltpu.CompilerParams(vmem_limit_bytes=62 << 20), name="pre",
    )(positions, segments, radius.reshape(1, 1024), currents, slot)
    col = lax.all_to_all(copies, "row", 0, 0, tiled=True)
    two = jnp.concatenate([block, swap(block, "col", 1)], 0)
    row = [two] + [swap(two, "col", 2 * m) for m in (1, 2, 3)]
    outs = pl.pallas_call(
        kernel, out_shape=(shape(2, 2, 1024),) * 4 + (shape(4, 2, 1024),) * 4,
        in_specs=[SM, SM] + [VM] * 5, out_specs=(VM,) * 8, scratch_shapes=SCRATCH,
        compiler_params=PARAMS, name="pairs",
    )(pair_list.T, near_flag, *row, col)
    a, b = outs[:4], outs[4:]
    b = [b[0]] + [swap(b[m], "row", 2 * m) for m in (1, 2, 3)]
    a = [a[0]] + [swap(a[m], "col", 2 * m) for m in (1, 2, 3)]
    b = (b[0] + b[1]) + (b[2] + b[3])
    a = (a[0] + a[1]) + (a[2] + a[3])
    b = b[0:2] + swap(b[2:4], "row", 8)
    parts = (a[0:1], swap(a[1:2], "col", 1), b[0:1], swap(b[1:2], "row", 1))
    return pl.pallas_call(
        post_kernel, out_shape=shape(2, 1024), in_specs=[VM] * 7, out_specs=VM,
        compiler_params=PARAMS, name="post",
    )(*parts, slot, resist.reshape(1, 1024), currents)


def solution(mesh):
    both = ("row", "col")
    return jax.shard_map(
        on_device, mesh=mesh,
        in_specs=(P_(None, both), P_(None, both), P_(both), P_(None, both), P_(both), P_(both),
                  P_(both, None), P_(both)),
        out_specs=P_(None, both), check_vma=False,
    )
```

```python
import math
import jax
import jax.numpy as jnp
from jax import lax
from jax.experimental import pallas as pl
from jax.experimental.pallas import tpu as pltpu
from jax.sharding import PartitionSpec as P_

CS = 512
G = 0.5 / math.sqrt(3.0)
f32, bf16 = jnp.float32, jnp.bfloat16
M = 256
FAR_UNROLL = 2


def split3(x):
    a = x.astype(bf16).astype(f32)
    r = x - a
    b = r.astype(bf16).astype(f32)
    return a, b, r - b


def rows8():
    return lax.broadcasted_iota(jnp.int32, (8, CS), 0)


def moved(P, L, s):
    if s == 0:
        return P, P[3:4]
    w = (G * L) * (2.0 * s * P + G * L)
    n = P[3:4] + ((w[0:1] + w[1:2]) + w[2:3])
    return P + (s * G) * L, n


def dist_tiles(P, L, s, first):
    Q, n = moved(P, L, s)
    r = rows8()
    if first:
        t = jnp.where(r < 3, -2.0 * Q, jnp.where(r == 3, n, jnp.where(r == 4, 1.0, 0.0)))
    else:
        t = jnp.where(r < 3, Q, jnp.where(r == 3, 1.0, jnp.where(r == 4, n, 0.0)))
    a, b, c = split3(t)
    if first:
        b = jnp.where(r == 4, 1.0, b)
        c = jnp.where(r == 4, 1.0, c)
        a5, b5 = pltpu.roll(a, 5, 0), pltpu.roll(b, 5, 0)
        return [jnp.where(r < 5, a, a5), jnp.where(r < 5, b, a5), jnp.where(r < 5, c, b5)]
    a5, b5, c5 = pltpu.roll(a, 5, 0), pltpu.roll(b, 5, 0), pltpu.roll(c, 5, 0)
    return [jnp.where(r < 5, a, b5),
            jnp.where(r < 4, a, jnp.where(r == 4, b, c5)),
            jnp.where(r < 4, a, jnp.where(r == 4, c, b5))]


def dot_tiles(L, scale, first):
    t = jnp.where(rows8() < 3, L * scale, 0.0)
    a, b, c = split3(t)
    a4, b4, c4 = (pltpu.roll(x, 4, 0) for x in (a, b, c))
    if first:
        return [a + a4, b + b4, a + c4]
    return [a + b4, a + b4, c + a4]


def load(ref, idx):
    dev = idx // 2
    h = idx % 2
    P = ref[dev, :, pl.ds(pl.multiple_of(h * CS, CS), CS)]
    ci = ref[dev, :, 1024:1152]
    ci = jnp.where(h == 1, pltpu.roll(ci, 4, 0), ci)
    return P, jnp.concatenate([ci[t:t + 1] for t in range(4)], 1)


def prep(ref, m, lt):
    zt = jnp.zeros((8, CS), f32)

    def step(i, _):
        for h in range(2):
            P = ref[i, :, CS * h:CS * h + CS]
            ci = ref[i, :, 1024:1152]
            ci = jnp.concatenate([ci[4 * h + t:4 * h + t + 1] for t in range(4)], 1)
            L = pltpu.roll(P, 4, 0)
            r = rows8()
            cur = jnp.where(r == 0, P[7:8], jnp.where(r == 1, ci, 0.0))
            tiles = (dist_tiles(P, L, 0, True) + [zt] + dist_tiles(P, L, 1.0, True) + [zt]
                     + dist_tiles(P, L, -1.0, True) + [zt] + dot_tiles(L, 0.25, True) + [cur])
            lt[4 * m + 2 * i + h] = jnp.concatenate(tiles, 0).T
        return 0

    for i in range(2):
        step(i, 0)


def kernel(pair_s, flag_s, w0, w1, w2, w3, col_ref, r0, r1, r2, r3, c0, c1, c2, c3,
           accd, accm, far_s, near_s, lt):
    me_row, me_col = pair_s[0, 0] >> 4, (pair_s[1, 0] >> 1) & 7
    nf = nn = jnp.int32(0)
    for k in range(32):
        I, J, fl = pair_s[0, k], pair_s[1, k], flag_s[k]
        code = ((I & 15) ^ (2 * me_col)) + ((J >> 4) * 2 + (J & 1)) * 16 + 512
        code = jnp.where(I == J, code, code + 1024)
        far_s[nf] = code
        near_s[nn] = code
        nf = nf + (fl == 1).astype(jnp.int32)
        nn = nn + (fl == 2).astype(jnp.int32)
    for m, ref in enumerate((w0, w1, w2, w3)):
        prep(ref, m, lt)
    accm[...] = jnp.zeros_like(accm)
    zt = jnp.zeros((8, CS), f32)

    def clear(i, _):
        accd[i] = jnp.zeros((CS, 256), f32)
        return 0
    lax.fori_loop(0, 16, clear, 0)

    for u in range(FAR_UNROLL):
        far_s[nf + u] = 0

    def open_pair(code, near):
        I, J = code & 15, (code >> 4) & 31
        wd = jnp.where(((code >> 9) & 1) == 1, 1.0, 0.0)
        wm = jnp.where((code >> 10) == 1, 1.0, 0.0)
        P, ci = load(col_ref, J)
        cr = P[7:8]
        L = pltpu.roll(P, 4, 0)
        z4 = [zt] * 4
        if near:
            vp = dist_tiles(P, L, 1.0, False) + [zt]
            vm = dist_tiles(P, L, -1.0, False) + [zt]
            mats = [z4 + vp + z4 + z4, z4 + z4 + vm + z4, z4 + vm + z4 + z4, z4 + z4 + vp + z4,
                    z4 * 3 + dot_tiles(L, 0.25, False) + [zt]]
            gain = 1.0
        else:
            mats = [dist_tiles(P, L, 0, False) + [zt] + z4 * 3,
                    z4 * 3 + dot_tiles(L, 1.0, False) + [zt]]
            gain = 1.0
        R = [jnp.concatenate(m, 0).astype(bf16) for m in mats]
        crs = [jnp.broadcast_to(cr[:, 128 * t:128 * t + 128] * (wd * gain), (8, 128)) for t in range(4)]
        cis = [jnp.broadcast_to(ci[:, 128 * t:128 * t + 128] * (wd * gain), (8, 128)) for t in range(4)]
        return dict(I=I, J=J, w=wm * gain, R=R, crs=crs, cis=cis, mr=[[None] * 4, [None] * 4])

    def advance(p, m, near):
        I, mr = p["I"], p["mr"]
        lhs = lt[I, m:m + M, :].astype(bf16)
        o = [jnp.dot(lhs, x, preferred_element_type=f32) for x in p["R"]]
        for q in range(0, M, 8):
            bc = lt[I, m + q:m + q + 8, :]
            br = jnp.broadcast_to(bc[:, 120:121], (8, 128))
            bi = jnp.broadcast_to(bc[:, 121:122], (8, 128))
            dr = di = None
            for t in range(4):
                x = [y[q:q + 8, 128 * t:128 * t + 128] for y in o]
                if near:
                    ri = (lax.rsqrt(x[0]) + lax.rsqrt(x[1])) + (lax.rsqrt(x[2]) + lax.rsqrt(x[3]))
                else:
                    ri = lax.rsqrt(x[0])
                g = ri * x[-1]
                a, b = g * p["crs"][t], g * p["cis"][t]
                dr = a if dr is None else dr + a
                di = b if di is None else di + b
                a, b = g * br, g * bi
                mr[0][t] = a if mr[0][t] is None else mr[0][t] + a
                mr[1][t] = b if mr[1][t] is None else mr[1][t] + b
            accd[I, m + q:m + q + 8, 0:128] += dr
            accd[I, m + q:m + q + 8, 128:256] += di

    def close_pair(p):
        for c in range(2):
            accm[p["J"], c] += p["w"] * jnp.concatenate(p["mr"][c], 1)

    def near_step(k, _):
        p = open_pair(near_s[k], True)
        for m in range(0, CS, M):
            advance(p, m, True)
        close_pair(p)
        return 0
    lax.fori_loop(0, nn, near_step, 0)

    def far_step(k, _):
        ps = [open_pair(far_s[FAR_UNROLL * k + u], False) for u in range(FAR_UNROLL)]
        for m in range(0, CS, M):
            for p in ps:
                advance(p, m, False)
        for p in ps:
            close_pair(p)
        return 0
    lax.fori_loop(0, (nf + FAR_UNROLL - 1) // FAR_UNROLL, far_step, 0)

    for m, out in enumerate((r0, r1, r2, r3)):
        for i in range(2):
            for h in range(2):
                x = accd[4 * m + 2 * i + h]
                for c in range(2):
                    t = x[:, 128 * c:128 * c + 128].T
                    out[i, c:c + 1, h * CS:(h + 1) * CS] = jnp.sum(t, 0, keepdims=True)

    for m, out in enumerate((c0, c1, c2, c3)):
        for k in range(4):
            slot = k // 2 * 8 + 2 * m + k % 2
            src = 2 * jnp.bitwise_xor(slot, me_row)
            for h in range(2):
                for c in range(2):
                    out[k, c:c + 1, h * CS:(h + 1) * CS] = jnp.sum(accm[src + h, c], 0, keepdims=True)


SCRATCH = [pltpu.VMEM((16, CS, 256), f32), pltpu.VMEM((32, 2, 8, CS), f32),
           pltpu.SMEM((40,), jnp.int32), pltpu.SMEM((40,), jnp.int32),
           pltpu.VMEM((16, CS, 128), f32)]


def pre_kernel(pos_hbm, seg_hbm, rad_hbm, cur_hbm, slot_hbm, one_ref, all_ref,
               pos_ref, seg_ref, rad_ref, cur_ref, slot_ref, sems):
    moves = [pltpu.make_async_copy(a, b, sems.at[i]) for i, (a, b) in enumerate(
        ((pos_hbm, pos_ref), (seg_hbm, seg_ref), (rad_hbm, rad_ref), (cur_hbm, cur_ref),
         (slot_hbm, slot_ref)))]
    out_ref = one_ref.at[0]
    for move in moves:
        move.start()
    for move in moves:
        move.wait()
    q = pos_ref[...] - 0.5
    a = rad_ref[...]
    n = (q[0:1] * q[0:1] + q[1:2] * q[1:2]) + (q[2:3] * q[2:3] + a * a)
    A = jnp.concatenate([q, n, seg_ref[...], cur_ref[0:1]], 0)
    B = cur_ref[1:2]
    a0, a1, a2 = split3(A)
    b0, b1, b2 = split3(B)
    X = jnp.concatenate([a0, a1, a2, b0, b1, b2, jnp.zeros((5, 1024), f32)], 0).astype(bf16)
    S = jnp.broadcast_to(slot_ref[...].astype(f32), (128, 1024)).T
    lane = lax.broadcasted_iota(jnp.int32, (1024, 128), 1).astype(f32)
    for g in range(0, 8, 2):
        hot = jnp.concatenate([jnp.where(S == lane + 128.0 * (g + i), 1.0, 0.0) for i in range(2)], 1)
        o = jnp.dot(X, hot.astype(bf16), preferred_element_type=f32)
        out_ref[:, 128 * g:128 * g + 256] = o[0:8] + o[8:16] + o[16:24]
        b = o[24:25] + o[25:26] + o[26:27]
        out_ref[g:g + 1, 1024:1152] = b[:, 0:128]
        out_ref[g + 1:g + 2, 1024:1152] = b[:, 128:256]
    for i in range(16):
        all_ref[i] = out_ref[...]


def post_kernel(a_ref, b_ref, c_ref, d_ref, slot_ref, res_ref, cur_ref, out_ref):
    s = (a_ref[0] + b_ref[0]) + (c_ref[0] + d_ref[0])
    p = jnp.concatenate([*split3(s), jnp.zeros((10, 1024), f32)], 0).astype(bf16)
    row = lax.broadcasted_iota(jnp.int32, (1024, 256), 0)
    for g in range(4):
        e = slice(256 * g, 256 * g + 256)
        hot = jnp.where(row == slot_ref[:, e], 1.0, 0.0).astype(bf16)
        o = jnp.dot(p, hot, preferred_element_type=f32)
        o = o[0:2] + o[2:4] + o[4:6]
        r = res_ref[:, e]
        out_ref[0:1, e] = r * cur_ref[0:1, e] - o[1:2]
        out_ref[1:2, e] = r * cur_ref[1:2, e] + o[0:1]


SM = pl.BlockSpec(memory_space=pltpu.SMEM)
VM = pl.BlockSpec(memory_space=pltpu.VMEM)
HB = pl.BlockSpec(memory_space=pltpu.HBM)
PARAMS = pltpu.CompilerParams(vmem_limit_bytes=24 << 20)


def shape(*dims):
    return jax.ShapeDtypeStruct(dims, f32)


def swap(value, axis, k):
    return lax.ppermute(value, axis, [(i, i ^ k) for i in range(lax.axis_size(axis))])


def on_device(positions, segments, radius, currents, resist, slot_of, pair_list, near_flag):
    slot = slot_of.reshape(1, 1024)
    block, copies = pl.pallas_call(
        pre_kernel, out_shape=(shape(1, 8, 1152), shape(16, 8, 1152)),
        in_specs=[HB] * 5, out_specs=(VM, VM),
        scratch_shapes=[pltpu.VMEM((3, 1024), f32), pltpu.VMEM((3, 1024), f32),
                        pltpu.VMEM((1, 1024), f32), pltpu.VMEM((2, 1024), f32),
                        pltpu.VMEM((1, 1024), jnp.int32), pltpu.SemaphoreType.DMA((5,))],
        compiler_params=pltpu.CompilerParams(vmem_limit_bytes=62 << 20), name="pre",
    )(positions, segments, radius.reshape(1, 1024), currents, slot)
    two = jnp.concatenate([block, swap(block, "col", 1)], 0)
    copies, two = lax.optimization_barrier((copies, two))
    col = lax.all_to_all(copies, "row", 0, 0, tiled=True)
    row = [two] + [swap(two, "col", 2 * m) for m in (1, 2, 3)]
    outs = pl.pallas_call(
        kernel, out_shape=(shape(2, 2, 1024),) * 4 + (shape(4, 2, 1024),) * 4,
        in_specs=[SM, SM] + [VM] * 5, out_specs=(VM,) * 8, scratch_shapes=SCRATCH,
        compiler_params=PARAMS, name="pairs",
    )(pair_list.T, near_flag, *row, col)
    a, b = outs[:4], outs[4:]
    b = [b[0]] + [swap(b[m], "row", 2 * m) for m in (1, 2, 3)]
    a = [a[0]] + [swap(a[m], "col", 2 * m) for m in (1, 2, 3)]
    b = (b[0] + b[1]) + (b[2] + b[3])
    a = (a[0] + a[1]) + (a[2] + a[3])
    b = b[0:2] + swap(b[2:4], "row", 8)
    parts = (a[0:1], swap(a[1:2], "col", 1), b[0:1], swap(b[1:2], "row", 1))
    return pl.pallas_call(
        post_kernel, out_shape=shape(2, 1024), in_specs=[VM] * 7, out_specs=VM,
        compiler_params=PARAMS, name="post",
    )(*parts, slot, resist.reshape(1, 1024), currents)


def solution(mesh):
    both = ("row", "col")
    return jax.shard_map(
        on_device, mesh=mesh,
        in_specs=(P_(None, both), P_(None, both), P_(both), P_(None, both), P_(both), P_(both),
                  P_(both, None), P_(both)),
        out_specs=P_(None, both), check_vma=False,
    )
```
